256 devices in a mesh: dp: 16 (over y, x_lo, core), tensor: 16 (over x_hi, z).
Axes of the slice: x: 4 (x_hi: 2, x_lo: 2; x = x_hi * 2 + x_lo), y: 4, z: 8, core: 2. Of those that a mesh axis runs over, the one named last changes fastest.
Arguments:
- x_rows: bfloat16 [512, 8192], P('tensor', 'dp'), may hold values from -6 to 6
- grad_out: bfloat16 [512, 8192], P('tensor', 'dp'), may hold values from -6 to 6
- order: int32 [512], replicated, may hold values from 0 to 511, each once
- gate_t: bfloat16 [28672, 8192], P('tensor', 'dp'), may hold values from -0.0625 to 0.0625
- up_t: bfloat16 [28672, 8192], P('tensor', 'dp'), may hold values from -0.0625 to 0.0625
- down_w: bfloat16 [28672, 8192], P('tensor', 'dp'), may hold values from -0.0625 to 0.0625
Outputs:
- grad_x: bfloat16 [512, 8192], P('tensor', 'dp')
- grad_gate: bfloat16 [28672, 8192], P('tensor', 'dp')
- grad_up: bfloat16 [28672, 8192], P('tensor', 'dp')
- grad_down: bfloat16 [28672, 8192], P('tensor', 'dp')
The draws below stay inside these ranges and needn't reach their ends.
Inputs may be any that keep to these rules, and one draw needn't show every extreme that they name: order is a permutation of 0 to 511.
All inputs are finite; a program needn't handle non-finite values.
Results may differ from the reference program's by a relative error of at most 0.0049.
Values may be sent and summed in bfloat16 or wider, within the bound.
A program may use at most 128 MiB of HBM per device.

```python
import jax
import jax.numpy as jnp
from jax import lax

D = 8192
FF = 28672
TOKENS = 512
N_TENSOR = 16


def block_levels(own_key, extent, cuts, low, top_value):
    loudness = 1.0
    for dim, shards_of in cuts:
        steps = jax.random.uniform(jax.random.fold_in(jax.random.fold_in(own_key, 6), dim), (shards_of,), jnp.float32, low / len(cuts), top_value / len(cuts))
        loudness = loudness * jnp.repeat(jnp.exp(steps), extent[dim] // shards_of).reshape((-1,) + (1,) * (len(extent) - 1 - dim))
    return loudness


def scatter_about(key, shape, spread, limit, pieces=(), held_as=jnp.bfloat16):
    values = spread * jax.random.normal(key, shape, jnp.float32)
    if pieces:
        values = values * block_levels(key, shape, pieces, -0.22, 0.18)
    return jnp.clip(values, -limit, limit).astype(held_as)


def setup_inputs(seed: int = 0) -> dict:
    seeds = jax.random.split(jax.random.key(seed), 7)
    x_rows = scatter_about(seeds[0], (TOKENS, D), 1.0, 6.0, ((0, 16), (1, 16)))
    grad_out = scatter_about(seeds[1], (TOKENS, D), 1.0, 6.0, ((0, 16), (1, 16)))
    order = jax.random.permutation(seeds[2], TOKENS).astype(jnp.int32)
    gate_t = scatter_about(seeds[3], (FF, D), D ** -0.5, 0.0625, ((0, 16), (1, 16)))
    up_t = scatter_about(seeds[4], (FF, D), D ** -0.5, 0.0625, ((0, 16), (1, 16)))
    down_w = scatter_about(seeds[5], (FF, D), D ** -0.5, 0.0625, ((0, 16), (1, 16)))
    return {"x_rows": x_rows, "grad_out": grad_out, "order": order, "gate_t": gate_t, "up_t": up_t, "down_w": down_w}


def reference(x_rows, grad_out, order, gate_t, up_t, down_w):
    xs = jnp.take(x_rows, order, axis=0)
    blocks = N_TENSOR
    width = FF // blocks

    def one_block(weights):
        g_w, u_w, d_w = weights
        gate = jnp.dot(xs, g_w.T, preferred_element_type=jnp.float32)
        up = jnp.dot(xs, u_w.T, preferred_element_type=jnp.float32)
        grad_hidden = jnp.dot(grad_out, d_w.T, preferred_element_type=jnp.float32)
        sig = jax.nn.sigmoid(gate)
        act = gate * sig
        hidden = (act * up).astype(jnp.bfloat16)
        grad_pre_gate = (grad_hidden * up * sig * (1.0 + gate * (1.0 - sig))).astype(jnp.bfloat16)
        grad_pre_up = (grad_hidden * act).astype(jnp.bfloat16)
        grad_down = jnp.dot(hidden.T, grad_out, preferred_element_type=jnp.float32).astype(jnp.bfloat16)
        grad_gate = jnp.dot(grad_pre_gate.T, xs, preferred_element_type=jnp.float32).astype(jnp.bfloat16)
        grad_up = jnp.dot(grad_pre_up.T, xs, preferred_element_type=jnp.float32).astype(jnp.bfloat16)
        cols = jnp.dot(grad_pre_gate, g_w, preferred_element_type=jnp.float32)
        cols = cols + jnp.dot(grad_pre_up, u_w, preferred_element_type=jnp.float32)
        return grad_gate, grad_up, grad_down, cols

    stacked = (gate_t.reshape(blocks, width, D), up_t.reshape(blocks, width, D), down_w.reshape(blocks, width, D))
    grad_gate, grad_up, grad_down, cols = lax.map(one_block, stacked)
    grad_xs = jnp.sum(cols, axis=0)
    grad_x = jnp.zeros_like(grad_xs).at[order].set(grad_xs).astype(jnp.bfloat16)
    return grad_x, grad_gate.reshape(FF, D), grad_up.reshape(FF, D), grad_down.reshape(FF, D)
```

```python
import functools

import jax
import jax.numpy as jnp
from jax import lax
from jax.experimental import pallas as pl
from jax.experimental.pallas import tpu as pltpu
from jax.sharding import PartitionSpec as P

MESH = pl.DeviceIdType.MESH
NY, NXL, NXH, NZ = 4, 2, 2, 8
CHUNKS = 7
ROWS = 128
SUB = 16
HALF_TOK = 256
TOK = 512
WIDE = 512
TB = 32
F32, BF16 = jnp.float32, jnp.bfloat16
Z_ORDER = (1, 7, 2, 6, 3, 5, 4)


def dot_nt(a, b):
    return lax.dot_general(a, b, (((1,), (1,)), ((), ())), preferred_element_type=F32)


def dot_nn(a, b):
    return lax.dot_general(a, b, (((1,), (0,)), ((), ())), preferred_element_type=F32)


def dot_tn(a, b):
    return lax.dot_general(a, b, (((0,), (0,)), ((), ())), preferred_element_type=F32)


def gated(pre):
    gate, up, grad_hidden = pre[0], pre[1], pre[2]
    sig = jax.nn.sigmoid(gate)
    act = gate * sig
    hidden = act * up
    grad_gate = grad_hidden * up * sig * (1.0 + gate * (1.0 - sig))
    grad_up = grad_hidden * act
    return jnp.stack([grad_gate, grad_up, hidden]).astype(BF16)


def kernel(
    x_hbm, dy_hbm, order_ref, wg, wu, wd,
    gx_out, gg_out, gu_out, gd_out,
    wall, wsib, xo, xs, dg, do, ds,
    pf_a, pf_b, pb_a, pb_b, rx_a, sb_a, ry_a, rb_b, s32_b, sb_b, rx_b,
    g_a, g_b, outs, gxa, gxb, gxr, gs32, gsb, gzr, gxf,
    c_send, c_recv, w_send, w_recv, l_sem, xz_send, xz_recv, xh_send, xh_recv,
    sib_send, sib_recv, o_sem, t_send, t_recv,
):
    dp = lax.axis_index("dp")
    tn = lax.axis_index("tensor")
    y, xl, k = dp // 4, (dp // 2) % 2, dp % 2
    xh, z = tn // 8, tn % 8

    def at(yy, xx, kk, hh, zz):
        return (yy * 4 + xx * 2 + kk, hh * 8 + zz)

    sibling = at(y, xl, 1 - k, xh, z)
    x_peer = at(y, 1 - xl, k, xh, z)
    h_peer = at(y, xl, k, 1 - xh, z)

    def y_peer(d):
        return at((y + d) % NY, xl, k, xh, z)

    def z_peer(d):
        return at(y, xl, k, xh, (z + d) % NZ)

    def rc(src, dst, send, recv, dev):
        return pltpu.make_async_remote_copy(
            src_ref=src, dst_ref=dst, send_sem=send, recv_sem=recv, device_id=dev, device_id_type=MESH
        )

    def load_w(j):
        src = (wg, wu, wd)[j]
        return pltpu.make_async_copy(src, wall.at[:, :, pl.ds(ROWS * j, ROWS)], l_sem.at[j])

    def send_w(j):
        src = (wg, wu, wd)[j]
        return rc(src.at[1 - k], wsib.at[:, pl.ds(ROWS * j, ROWS)], w_send.at[j], w_recv.at[j], sibling)

    def load_x():
        return pltpu.make_async_copy(x_hbm, xo.at[tn], l_sem.at[3])

    def load_dy():
        return pltpu.make_async_copy(dy_hbm, dg.at[tn], l_sem.at[4])

    def gather_z(j, d):
        src, dst = ((x_hbm, xo), (dy_hbm, dg))[j]
        return rc(src, dst.at[tn], xz_send.at[j, d], xz_recv.at[j, d], z_peer(d))

    def gather_h(j, d):
        dst = (xo, dg)[j]
        block = xh * NZ + (z + NZ - d) % NZ
        return rc(dst.at[block], dst.at[block], xh_send.at[j, d], xh_recv.at[j, d], h_peer)

    def swap_x():
        return rc(xo, xs, sib_send.at[0], sib_recv.at[0], sibling)

    def swap_dy():
        return rc(do, ds, sib_send.at[1], sib_recv.at[1], sibling)

    def cc(i, n, src, dst, dev):
        return rc(src, dst, c_send.at[i, n], c_recv.at[i, n], dev)

    def a1(i):
        return cc(i, 0, pb_a.at[i, :, 1 - xl], rx_a.at[i], x_peer)

    def a2(i, d):
        return cc(i, d, sb_a.at[i, :, (y + d) % NY], ry_a.at[i, d - 1], y_peer(d))

    def b1(i, d):
        return cc(i, 3 + d, pb_b.at[i, :, :, (y + d) % NY], rb_b.at[i, d - 1], y_peer(d))

    def b2(i):
        return cc(i, 7, sb_b.at[i], rx_b.at[i], x_peer)

    def ga1(i, d):
        ref = g_a.at[k, i, :, xl, y]
        return cc(i, 7 + d, ref, ref, y_peer(d))

    def ga2(i):
        ref = g_a.at[k, i, :, xl]
        return cc(i, 11, ref, ref, x_peer)

    def gb1(i):
        ref = g_b.at[k, i, :, xl, y]
        return cc(i, 12, ref, ref, x_peer)

    def gb2(i, d):
        ref = g_b.at[k, i, :, :, y]
        return cc(i, 12 + d, ref, ref, y_peer(d))

    def sw1(i):
        ref = g_a.at[k, i, :, xl]
        return cc(i, 16, ref, ref, sibling)

    def sw2(i):
        ref = g_a.at[k, i, :, 1 - xl]
        return cc(i, 17, ref, ref, sibling)

    def sw3(i):
        ref = g_b.at[k, i]
        return cc(i, 18, ref, ref, sibling)

    def write_out(i, h, j):
        dst = (gg_out, gu_out, gd_out)[j]
        return pltpu.make_async_copy(outs.at[h, i, pl.ds(ROWS * j, ROWS)], dst.at[h, i], o_sem.at[i, h, j])

    def tail_h():
        return rc(gxb.at[1 - xh], gxr, t_send.at[0], t_recv.at[0], h_peer)

    def tail_z(d):
        return rc(gsb.at[(z + d) % NZ], gzr.at[d - 1], t_send.at[d], t_recv.at[d], z_peer(d))

    load_x().start()
    load_dy().start()
    for j in range(3):
        load_w(j).start()
    barrier = pltpu.get_barrier_semaphore()
    partners = [sibling, x_peer, h_peer]
    partners += [y_peer(d) for d in range(1, NY)] + [z_peer(d) for d in range(1, NZ)]
    for dev in partners:
        pl.semaphore_signal(barrier, inc=1, device_id=dev, device_id_type=MESH)
    pl.semaphore_wait(barrier, len(partners))

    for j in range(2):
        for d in Z_ORDER:
            gather_z(j, d).start()
    for j in range(3):
        send_w(j).start()
    gxa[...] = jnp.zeros_like(gxa)

    for j in range(2):
        (load_x, load_dy)[j]().wait()
        gather_h(j, 0).start()
        for d in Z_ORDER:
            gather_z(j, d).wait_recv()
            gather_h(j, d).start()
        for d in range(NZ):
            gather_h(j, d).wait_recv()
        if j == 0:
            swap_x().start()
    rows = lax.broadcasted_iota(jnp.int32, (TOK, TOK), 0)
    place = jnp.where(rows == order_ref[...], 1.0, 0.0).astype(BF16)
    do[...] = dot_nn(place, dg[...].reshape(TOK, WIDE)).astype(BF16).reshape(NXH * NZ, TB, WIDE)
    swap_dy().start()
    for j in range(3):
        load_w(j).wait()
        send_w(j).wait_recv()
    swap_x().wait_recv()
    swap_dy().wait_recv()

    def flat(ref):
        return ref[...].reshape(TOK, WIDE)

    def forward(i):
        gu = dot_nt(wall[k, i, : 2 * ROWS], flat(xo)) + dot_nt(wsib[i, : 2 * ROWS], flat(xs))
        gh = dot_nt(wall[k, i, 2 * ROWS :], flat(do)) + dot_nt(wsib[i, 2 * ROWS :], flat(ds))
        for pf, pb, lo in ((pf_a, pb_a, 0), (pf_b, pb_b, HALF_TOK)):
            part_gu = gu[:, lo : lo + HALF_TOK].reshape(2, NXL, NY, SUB, HALF_TOK)
            part_gh = gh[:, lo : lo + HALF_TOK].reshape(NXL, NY, SUB, HALF_TOK)
            pf[i, 0:2] = part_gu
            pf[i, 2] = part_gh
            pb[i, 0:2] = part_gu.astype(BF16)
            pb[i, 2] = part_gh.astype(BF16)
        a1(i).start()
        for d in range(1, NY):
            b1(i, d).start()

    def reduce_one(i):
        a1(i).wait_recv()
        sb_a[i] = (pf_a[i, :, xl] + rx_a[i].astype(F32)).astype(BF16)
        for d in range(1, NY):
            a2(i, d).start()
        total = pf_b[i, :, :, y]
        for d in range(1, NY):
            b1(i, d).wait_recv()
            total = total + rb_b[i, d - 1].astype(F32)
        s32_b[i] = total
        sb_b[i] = s32_b[i, :, 1 - xl].astype(BF16)
        b2(i).start()

    def reduce_two(i):
        total = pf_a[i, :, xl, y] + rx_a[i, :, y].astype(F32)
        for d in range(1, NY):
            a2(i, d).wait_recv()
            total = total + ry_a[i, d - 1].astype(F32)
        g_a[k, i, :, xl, y] = gated(total)
        for d in range(1, NY):
            ga1(i, d).start()
        b2(i).wait_recv()
        g_b[k, i, :, xl, y] = gated(s32_b[i, :, xl] + rx_b[i].astype(F32))
        gb1(i).start()

    def gather_one(i):
        gb1(i).wait_recv()
        for d in range(1, NY):
            gb2(i, d).start()
        for d in range(1, NY):
            ga1(i, d).wait_recv()
        ga2(i).start()
        sw1(i).start()

    def gather_two(i):
        ga2(i).wait_recv()
        sw2(i).start()
        for d in range(1, NY):
            gb2(i, d).wait_recv()
        sw3(i).start()

    def backward(i):
        for sw in (sw1, sw2, sw3):
            sw(i).wait_recv()
        for h in range(2):
            for n, g in ((0, g_a), (1, g_b)):
                gxa[n] += dot_tn(
                    g[h, i, 0:2].reshape(2 * ROWS, HALF_TOK), wall[h, i, : 2 * ROWS]
                ).reshape(NZ, TB, WIDE)

    def backward_w(i):
        half = (NZ * TB, WIDE)
        for h in range(2):
            gu = dot_nn(g_a[h, i, 0:2].reshape(2 * ROWS, HALF_TOK), xo[:NZ].reshape(half))
            gu = gu + dot_nn(g_b[h, i, 0:2].reshape(2 * ROWS, HALF_TOK), xo[NZ:].reshape(half))
            gd = dot_nn(g_a[h, i, 2].reshape(ROWS, HALF_TOK), do[:NZ].reshape(half))
            gd = gd + dot_nn(g_b[h, i, 2].reshape(ROWS, HALF_TOK), do[NZ:].reshape(half))
            outs[h, i, : 2 * ROWS] = gu.astype(BF16)
            outs[h, i, 2 * ROWS :] = gd.astype(BF16)
            for j in range(3):
                write_out(i, h, j).start()

    steps = (forward, reduce_one, reduce_two, gather_one, gather_two, backward)
    after = (0, 1, 2, 3, 4, 5)

    def turn(it, _):
        for step, lag in zip(steps, after):
            i = it - lag

            @pl.when((i >= 0) & (i < CHUNKS))
            def _():
                step(i)

        i = it - after[-1]

        @pl.when((i >= 0) & (i < CHUNKS - 1))
        def _():
            backward_w(i)

        return 0

    lax.fori_loop(0, CHUNKS + after[-1], turn, 0)

    gxb[...] = gxa[...].astype(BF16)
    tail_h().start()
    backward_w(CHUNKS - 1)
    tail_h().wait_recv()
    gs32[...] = gxa[xh] + gxr[...].astype(F32)
    gsb[...] = gs32[...].astype(BF16)
    for d in Z_ORDER:
        tail_z(d).start()
    total = gs32[z]
    for d in Z_ORDER:
        tail_z(d).wait_recv()
        total = total + gzr[d - 1].astype(F32)
    gxf[...] = total.astype(BF16)
    done = pltpu.make_async_copy(gxf, gx_out, l_sem.at[5])
    done.start()

    for j in range(3):
        send_w(j).wait_send()
    for j in range(2):
        for d in range(1, NZ):
            gather_z(j, d).wait_send()
        for d in range(NZ):
            gather_h(j, d).wait_send()
    swap_x().wait_send()
    swap_dy().wait_send()

    def drain(i, _):
        for c in (a1(i), b2(i), ga2(i), gb1(i), sw1(i), sw2(i), sw3(i)):
            c.wait_send()
        for d in range(1, NY):
            for c in (a2(i, d), b1(i, d), ga1(i, d), gb2(i, d)):
                c.wait_send()
        for h in range(2):
            for j in range(3):
                write_out(i, h, j).wait()
        return 0

    lax.fori_loop(0, CHUNKS, drain, 0)
    tail_h().wait_send()
    for d in range(1, NZ):
        tail_z(d).wait_send()
    done.wait()


def per_device(x_rows, grad_out, order, gate_t, up_t, down_w):
    weight = (2, CHUNKS, ROWS, WIDE)
    any_spec = pl.BlockSpec(memory_space=pl.ANY)
    dma = pltpu.SemaphoreType.DMA
    n = CHUNKS
    vm = pltpu.VMEM
    scratch = [
        vm((2, n, 3 * ROWS, WIDE), BF16),
        vm((n, 3 * ROWS, WIDE), BF16),
        vm((16, TB, WIDE), BF16),
        vm((16, TB, WIDE), BF16),
        vm((16, TB, WIDE), BF16),
        vm((16, TB, WIDE), BF16),
        vm((16, TB, WIDE), BF16),
        vm((n, 3, NXL, NY, SUB, HALF_TOK), F32),
        vm((n, 3, NXL, NY, SUB, HALF_TOK), F32),
        vm((n, 3, NXL, NY, SUB, HALF_TOK), BF16),
        vm((n, 3, NXL, NY, SUB, HALF_TOK), BF16),
        vm((n, 3, NY, SUB, HALF_TOK), BF16),
        vm((n, 3, NY, SUB, HALF_TOK), BF16),
        vm((n, 3, 3, SUB, HALF_TOK), BF16),
        vm((n, 3, 3, NXL, SUB, HALF_TOK), BF16),
        vm((n, 3, NXL, SUB, HALF_TOK), F32),
        vm((n, 3, SUB, HALF_TOK), BF16),
        vm((n, 3, SUB, HALF_TOK), BF16),
        vm((2, n, 3, NXL, NY, SUB, HALF_TOK), BF16),
        vm((2, n, 3, NXL, NY, SUB, HALF_TOK), BF16),
        vm((2, n, 3 * ROWS, WIDE), BF16),
        vm((NXH, NZ, TB, WIDE), F32),
        vm((NXH, NZ, TB, WIDE), BF16),
        vm((NZ, TB, WIDE), BF16),
        vm((NZ, TB, WIDE), F32),
        vm((NZ, TB, WIDE), BF16),
        vm((NZ - 1, TB, WIDE), BF16),
        vm((TB, WIDE), BF16),
        dma((n, 19)), dma((n, 19)),
        dma((3,)), dma((3,)),
        dma((6,)),
        dma((2, NZ)), dma((2, NZ)),
        dma((2, NZ)), dma((2, NZ)),
        dma((2,)), dma((2,)),
        dma((n, 2, 3)),
        dma((NZ,)), dma((NZ,)),
    ]
    out = pl.pallas_call(
        kernel,
        out_shape=[jax.ShapeDtypeStruct((TB, WIDE), BF16)]
        + [jax.ShapeDtypeStruct(weight, BF16)] * 3,
        in_specs=[any_spec, any_spec, pl.BlockSpec(memory_space=pltpu.VMEM)] + [any_spec] * 3,
        out_specs=[any_spec] * 4,
        scratch_shapes=scratch,
        compiler_params=pltpu.CompilerParams(
            collective_id=0, has_side_effects=True, vmem_limit_bytes=56 * 2**20
        ),
        name="ffn_backward",
    )(
        x_rows, grad_out, order.reshape(1, TOK),
        gate_t.reshape(weight), up_t.reshape(weight), down_w.reshape(weight),
    )
    full = gate_t.shape
    return out[0], out[1].reshape(full), out[2].reshape(full), out[3].reshape(full)


def solution(mesh):
    return jax.shard_map(
        per_device,
        mesh=mesh,
        in_specs=(
            P("tensor", "dp"),
            P("tensor", "dp"),
            P(),
            P("tensor", "dp"),
            P("tensor", "dp"),
            P("tensor", "dp"),
        ),
        out_specs=(P("tensor", "dp"), P("tensor", "dp"), P("tensor", "dp"), P("tensor", "dp")),
        check_vma=False,
    )
```

```python
from types import SimpleNamespace

import jax
import jax.numpy as jnp
from jax import lax
from jax.experimental import pallas as pl
from jax.experimental.pallas import tpu as pltpu
from jax.sharding import PartitionSpec as P

MESH = pl.DeviceIdType.MESH
NY, NXL, NXH, NZ = 4, 2, 2, 8
CHUNKS = 7
ROWS = 128
SUB = 16
HALF = 256
TOK = 512
WIDE = 512
TB = 32
F32, BF16 = jnp.float32, jnp.bfloat16
Z_ORDER = (1, 7, 2, 6, 3, 5, 4)
Y_ALL = (1, 3, 2)
WEIGHT = (2, CHUNKS, ROWS, WIDE)


def dot_nt(a, b):
    return lax.dot_general(a, b, (((1,), (1,)), ((), ())), preferred_element_type=F32)


def dot_nn(a, b):
    return lax.dot_general(a, b, (((1,), (0,)), ((), ())), preferred_element_type=F32)


def dot_tn(a, b):
    return lax.dot_general(a, b, (((0,), (0,)), ((), ())), preferred_element_type=F32)


def scratch_plan():
    n = CHUNKS
    cell = (SUB, HALF)
    plan = [
        ("wall", (2, n, 3 * ROWS, WIDE), BF16),
        ("wsib", (n, 3 * ROWS, WIDE), BF16),
        ("xo", (NXH, NZ, TB, WIDE), BF16),
        ("xs", (NXH, NZ, TB, WIDE), BF16),
        ("dg", (NXH, NZ, TB, WIDE), BF16),
        ("do", (NXH, NZ, TB, WIDE), BF16),
        ("ds", (NXH, NZ, TB, WIDE), BF16),
        ("place", (TOK, TOK), BF16),
    ]
    for s, nf in (("u", 2), ("d", 1)):
        grid = (n, nf, NXL, NY) + cell
        plan += [
            (s + "_pf_a", grid, F32),
            (s + "_pf_b", grid, F32),
            (s + "_pb_a", grid, BF16),
            (s + "_pb_b", grid, BF16),
            (s + "_rx_a", (n, nf, NY) + cell, BF16),
            (s + "_sb_a", (n, nf, NY) + cell, BF16),
            (s + "_ry_a", (n, 3, nf) + cell, BF16),
            (s + "_r0_b", (n, 2, nf) + cell, BF16),
            (s + "_f_b", (n, 2, nf, NXL) + cell, BF16),
            (s + "_r1_b", (n, 2, nf, NXL) + cell, BF16),
            (s + "_s_b", (n, nf, NXL) + cell, F32),
            (s + "_sb_b", (n, nf) + cell, BF16),
            (s + "_rx_b", (n, nf) + cell, BF16),
            (s + "_send", (n, 9), None),
            (s + "_recv", (n, 9), None),
        ]
    plan += [
        ("t_a", (n, 2) + cell, F32),
        ("t_b", (n, 2) + cell, F32),
        ("g_a", (2, n, 2, NXL, NY) + cell, BF16),
        ("g_b", (2, n, 2, NXL, NY) + cell, BF16),
        ("h_a", (2, n, NXL, NY) + cell, BF16),
        ("h_b", (2, n, NXL, NY) + cell, BF16),
        ("gxa", (NXH, NZ, TB, WIDE), F32),
        ("es", (NXH, TB, HALF), F32),
        ("esr", (TB, HALF), F32),
        ("gxb", (2, NXH, NZ, TB, HALF), BF16),
        ("gxr", (NZ, TB, HALF), BF16),
        ("gs", (NZ, TB, HALF), F32),
        ("gsb", (NZ, TB, HALF), BF16),
        ("gz1", (NZ - 1, TB, HALF), BF16),
        ("gz2", (NZ - 1, NXH, TB, HALF), BF16),
        ("g_send", (n, 12), None),
        ("g_recv", (n, 12), None),
        ("h_send", (11,), None),
        ("h_recv", (11,), None),
        ("w_send", (3,), None),
        ("w_recv", (3,), None),
        ("l_sem", (5,), None),
        ("xz_send", (2, NZ), None),
        ("xz_recv", (2, NZ), None),
        ("xh_send", (NZ + 1,), None),
        ("xh_recv", (NZ + 1,), None),
        ("sib_send", (3,), None),
        ("sib_recv", (3,), None),
        ("t_send", (2 * NZ,), None),
        ("t_recv", (2 * NZ,), None),
    ]
    return plan


def kernel(x_hbm, dy_hbm, order_ref, wg, wu, wd, gx_ref, outs, *scratch):
    m = SimpleNamespace(**{p[0]: ref for p, ref in zip(scratch_plan(), scratch)})
    dp = lax.axis_index("dp")
    tn = lax.axis_index("tensor")
    y, xl, k = dp // 4, (dp // 2) % 2, dp % 2
    xh, z = tn // NZ, tn % NZ

    def at(yy, xx, kk, hh, zz):
        return (yy * 4 + xx * 2 + kk, hh * NZ + zz)

    sibling = at(y, xl, 1 - k, xh, z)
    x_peer = at(y, 1 - xl, k, xh, z)
    h_peer = at(y, xl, k, 1 - xh, z)

    def y_at(d):
        return (y + d) % NY

    def y_peer(d):
        return at(y_at(d), xl, k, xh, z)

    def z_peer(d):
        return at(y, xl, k, xh, (z + d) % NZ)

    def rc(src, dst, send, recv, dev):
        return pltpu.make_async_remote_copy(
            src_ref=src, dst_ref=dst, send_sem=send, recv_sem=recv, device_id=dev, device_id_type=MESH
        )

    def load_w(j):
        return pltpu.make_async_copy(
            (wg, wu, wd)[j], m.wall.at[:, :, pl.ds(ROWS * j, ROWS)], m.l_sem.at[j]
        )

    def send_w(j):
        dst = m.wsib.at[:, pl.ds(ROWS * j, ROWS)]
        return rc((wg, wu, wd)[j].at[1 - k], dst, m.w_send.at[j], m.w_recv.at[j], sibling)

    def load_x():
        return pltpu.make_async_copy(x_hbm, m.xo.at[xh, z], m.l_sem.at[3])

    def load_dy():
        return pltpu.make_async_copy(dy_hbm, m.dg.at[xh, z], m.l_sem.at[4])

    def x_z(d):
        return rc(x_hbm, m.xo.at[xh, z], m.xz_send.at[0, d], m.xz_recv.at[0, d], z_peer(d))

    def x_h(d):
        block = m.xo.at[xh, (z + NZ - d) % NZ]
        return rc(block, block, m.xh_send.at[d], m.xh_recv.at[d], h_peer)

    def dy_h():
        return rc(dy_hbm, m.dg.at[xh, z], m.xh_send.at[NZ], m.xh_recv.at[NZ], h_peer)

    def dy_z(d):
        pair = m.dg.at[:, z]
        return rc(pair, pair, m.xz_send.at[1, d], m.xz_recv.at[1, d], z_peer(d))

    def swap_x(part):
        half = (xh, 1 - xh)[part]
        return rc(m.xo.at[half], m.xs.at[half], m.sib_send.at[part], m.sib_recv.at[part], sibling)

    def swap_dy():
        return rc(m.do, m.ds, m.sib_send.at[2], m.sib_recv.at[2], sibling)

    def stream(s, nf):
        pre = s + "_"
        q = SimpleNamespace(
            **{key[len(pre) :]: ref for key, ref in vars(m).items() if key.startswith(pre)}
        )

        def cc(i, c, src, dst, dev):
            return rc(src, dst, q.send.at[i, c], q.recv.at[i, c], dev)

        def a1(i):
            return cc(i, 0, q.pb_a.at[i, :, 1 - xl], q.rx_a.at[i], x_peer)

        def a2(i, d):
            return cc(i, d, q.sb_a.at[i, :, y_at(d)], q.ry_a.at[i, d - 1], y_peer(d))

        def b0(i, w):
            return cc(i, 4 + w, q.pb_b.at[i, :, w, y_at(2)], q.r0_b.at[i, w], y_peer((1, 3)[w]))

        def b1(i, w):
            return cc(i, 6 + w, q.f_b.at[i, w], q.r1_b.at[i, w], y_peer((1, 3)[w]))

        def b2(i):
            return cc(i, 8, q.sb_b.at[i], q.rx_b.at[i], x_peer)

        def begin(i, parts):
            for pf, pb, lo in ((q.pf_a, q.pb_a, 0), (q.pf_b, q.pb_b, HALF)):
                part = parts[:, lo : lo + HALF].reshape(nf, NXL, NY, SUB, HALF)
                pf[i] = part
                pb[i] = part.astype(BF16)
            a1(i).start()
            for w in range(2):
                b0(i, w).start()

        def first(i):
            for w in range(2):
                b0(i, w).wait_recv()
                to = y_at((1, 3)[w])
                q.f_b[i, w, :, w] = (q.pf_b[i, :, w, to] + q.r0_b[i, w].astype(F32)).astype(BF16)
                q.f_b[i, w, :, 1 - w] = q.pb_b[i, :, 1 - w, to]
                b1(i, w).start()
            a1(i).wait_recv()
            q.sb_a[i] = (q.pf_a[i, :, xl] + q.rx_a[i].astype(F32)).astype(BF16)
            for d in Y_ALL:
                a2(i, d).start()

        def sum_a(i):
            total = q.pf_a[i, :, xl, y] + q.rx_a[i, :, y].astype(F32)
            for d in Y_ALL:
                a2(i, d).wait_recv()
                total = total + q.ry_a[i, d - 1].astype(F32)
            return total

        def second_b(i):
            total = q.pf_b[i, :, :, y]
            for w in range(2):
                b1(i, w).wait_recv()
                total = total + q.r1_b[i, w].astype(F32)
            q.s_b[i] = total
            q.sb_b[i] = q.s_b[i, :, 1 - xl].astype(BF16)
            b2(i).start()

        def sum_b(i):
            b2(i).wait_recv()
            return q.s_b[i, :, xl] + q.rx_b[i].astype(F32)

        def sent(i):
            cs = [a1(i), b2(i)] + [a2(i, d) for d in Y_ALL]
            return cs + [b(i, w) for b in (b0, b1) for w in range(2)]

        return SimpleNamespace(
            begin=begin, first=first, sum_a=sum_a, second_b=second_b, sum_b=sum_b, sent=sent
        )

    up_stream, dy_stream = stream("u", 2), stream("d", 1)

    def cg(i, c, src, dev):
        return rc(src, src, m.g_send.at[i, c], m.g_recv.at[i, c], dev)

    def ga1(i, d):
        return cg(i, d - 1, m.g_a.at[k, i, :, xl, y], y_peer(d))

    def ga2(i):
        return cg(i, 3, m.g_a.at[k, i, :, xl], x_peer)

    def gb1(i):
        return cg(i, 4, m.g_b.at[k, i, :, xl, y], x_peer)

    def gb2(i, w):
        return cg(i, 5 + w, m.g_b.at[k, i, :, :, y], y_peer((1, 3)[w]))

    def gb3(i, w):
        return cg(i, 7 + w, m.g_b.at[k, i, :, w, y_at((3, 1)[w])], y_peer((1, 3)[w]))

    def sw(i, part):
        src = (m.g_a.at[k, i, :, xl], m.g_a.at[k, i, :, 1 - xl], m.g_b.at[k, i])[part]
        return cg(i, 9 + part, src, sibling)

    def ch(c, src, dev):
        return rc(src, src, m.h_send.at[c], m.h_recv.at[c], dev)

    def ha1(d):
        return ch(d - 1, m.h_a.at[k, :, xl, y], y_peer(d))

    def ha2():
        return ch(3, m.h_a.at[k, :, xl], x_peer)

    def hb1():
        return ch(4, m.h_b.at[k, :, xl, y], x_peer)

    def hb2(d):
        return ch(4 + d, m.h_b.at[k, :, :, y], y_peer(d))

    def hsw(part):
        src = (m.h_a.at[k, :, xl], m.h_a.at[k, :, 1 - xl], m.h_b.at[k])[part]
        return ch(8 + part, src, sibling)

    def ct(c, src, dst, dev):
        return rc(src, dst, m.t_send.at[c], m.t_recv.at[c], dev)

    def tail_h():
        return ct(0, m.gxb.at[0, 1 - xh], m.gxr, h_peer)

    def tail_z1(d):
        return ct(d, m.gsb.at[(z + d) % NZ], m.gz1.at[d - 1], z_peer(d))

    def tail_z2(d):
        return ct(NZ + d, m.gxb.at[1, :, (z + d) % NZ], m.gz2.at[d - 1], z_peer(d))

    def tail_h2():
        return ct(NZ, m.es.at[1 - xh], m.esr, h_peer)

    load_x().start()
    load_dy().start()
    for j in range(3):
        load_w(j).start()
    barrier = pltpu.get_barrier_semaphore()
    partners = [z_peer(d) for d in range(1, NZ)] + [y_peer(d) for d in range(1, NY)]
    partners += [h_peer, x_peer, sibling]
    for dev in partners:
        pl.semaphore_signal(barrier, inc=1, device_id=dev, device_id_type=MESH)
    pl.semaphore_wait(barrier, len(partners))

    for d in Z_ORDER:
        x_z(d).start()
    load_x().wait()
    x_h(0).start()
    dy_h().start()
    for j in range(3):
        send_w(j).start()
    m.gxa[...] = jnp.zeros_like(m.gxa)
    rows = lax.broadcasted_iota(jnp.int32, (TOK, TOK), 0)
    m.place[...] = jnp.where(rows == order_ref[...], 1.0, 0.0).astype(BF16)
    for d in Z_ORDER:
        x_z(d).wait_recv()
        x_h(d).start()
    swap_x(0).start()
    load_dy().wait()
    dy_h().wait_recv()
    for d in Z_ORDER:
        dy_z(d).start()
    for d in range(NZ):
        x_h(d).wait_recv()
    swap_x(1).start()
    for j in range(2):
        load_w(j).wait()
        send_w(j).wait_recv()
    for part in range(2):
        swap_x(part).wait_recv()

    def flat(ref):
        return ref[...].reshape(TOK, WIDE)

    def prepare_dy():
        for d in Z_ORDER:
            dy_z(d).wait_recv()
        m.do[...] = dot_nn(m.place[...], flat(m.dg)).astype(BF16).reshape(NXH, NZ, TB, WIDE)
        swap_dy().start()

    def forward_u(i):
        up_stream.begin(
            i,
            dot_nt(m.wall[k, i, : 2 * ROWS], flat(m.xo)) + dot_nt(m.wsib[i, : 2 * ROWS], flat(m.xs)),
        )

    def forward_d(i):
        dy_stream.begin(
            i,
            dot_nt(m.wall[k, i, 2 * ROWS :], flat(m.do)) + dot_nt(m.wsib[i, 2 * ROWS :], flat(m.ds)),
        )

    def hidden_of(i, total, t, h):
        t[i] = total
        gate, up = total[0], total[1]
        h[k, i, xl, y] = (gate * jax.nn.sigmoid(gate) * up).astype(BF16)

    def second_u(i):
        hidden_of(i, up_stream.sum_a(i), m.t_a, m.h_a)
        up_stream.second_b(i)

    def third_u(i):
        hidden_of(i, up_stream.sum_b(i), m.t_b, m.h_b)

    def gated(i, grad_hidden, t, g):
        gate, up = t[i, 0], t[i, 1]
        sig = jax.nn.sigmoid(gate)
        grad_gate = grad_hidden * up * sig * (1.0 + gate * (1.0 - sig))
        grad_up = grad_hidden * (gate * sig)
        g[k, i, 0, xl, y] = grad_gate.astype(BF16)
        g[k, i, 1, xl, y] = grad_up.astype(BF16)

    def second_d(i):
        gated(i, dy_stream.sum_a(i)[0], m.t_a, m.g_a)
        for d in Y_ALL:
            ga1(i, d).start()
        dy_stream.second_b(i)

    def third_d(i):
        gated(i, dy_stream.sum_b(i)[0], m.t_b, m.g_b)
        gb1(i).start()

    def gather_a1(i):
        for d in Y_ALL:
            ga1(i, d).wait_recv()
        ga2(i).start()
        sw(i, 0).start()

    def gather_b1(i):
        gb1(i).wait_recv()
        for w in range(2):
            gb2(i, w).start()

    def gather_a2(i):
        ga2(i).wait_recv()
        sw(i, 1).start()

    def gather_b2(i):
        for w in range(2):
            gb2(i, w).wait_recv()
            gb3(i, w).start()

    def gather_b3(i):
        for w in range(2):
            gb3(i, w).wait_recv()
        sw(i, 2).start()

    def backward(i, p, g):
        for h in range(2):
            m.gxa[p] += dot_tn(
                g[h, i].reshape(2 * ROWS, HALF), m.wall[h, i, : 2 * ROWS]
            ).reshape(NZ, TB, WIDE)

    def backward_a(i):
        for part in range(2):
            sw(i, part).wait_recv()
        backward(i, 0, m.g_a)

    def backward_b(i):
        sw(i, 2).wait_recv()
        backward(i, 1, m.g_b)

    def backward_w(i):
        for h in range(2):
            gu = dot_nn(m.g_a[h, i].reshape(2 * ROWS, HALF), m.xo[0].reshape(HALF, WIDE))
            gu = gu + dot_nn(m.g_b[h, i].reshape(2 * ROWS, HALF), m.xo[1].reshape(HALF, WIDE))
            outs[h, i, : 2 * ROWS] = gu.astype(BF16)

    def backward_d(i):
        for h in range(2):
            gd = dot_nn(m.h_a[h, i].reshape(ROWS, HALF), m.do[0].reshape(HALF, WIDE))
            gd = gd + dot_nn(m.h_b[h, i].reshape(ROWS, HALF), m.do[1].reshape(HALF, WIDE))
            outs[h, i, 2 * ROWS :] = gd.astype(BF16)

    end = CHUNKS - 1

    def each(*steps, lo=0, hi=CHUNKS):
        most = max(lag for _, lag in steps)

        def turn(it, _):
            for step, lag in steps:
                i = it - lag
                if most == 0:
                    step(i)
                    continue

                @pl.when((i >= lo) & (i < hi))
                def _():
                    step(i)

            return 0

        lax.fori_loop(lo, hi + most, turn, 0)

    each((forward_u, 0))
    each((up_stream.first, 0), lo=0, hi=5)
    prepare_dy()
    each((up_stream.first, 0), lo=5, hi=CHUNKS)
    load_w(2).wait()
    send_w(2).wait_recv()
    swap_dy().wait_recv()
    each((forward_d, 0))
    each((second_u, 0))
    each((dy_stream.first, 0))
    each((third_u, 0))
    each((second_d, 0))
    each((third_d, 0))
    each((gather_a1, 0))
    each((gather_b1, 0))
    each((gather_b2, 0))
    for d in Y_ALL:
        ha1(d).start()
    hb1().start()
    each((gather_a2, 0))
    each((gather_b3, 0))
    each((backward_a, 0))
    each((backward_b, 0))
    m.gxb[0] = m.gxa[:, :, :, :HALF].astype(BF16)
    m.gxb[1] = m.gxa[:, :, :, HALF:].astype(BF16)
    tail_h().start()
    for d in Z_ORDER:
        tail_z2(d).start()
    for d in Y_ALL:
        ha1(d).wait_recv()
    ha2().start()
    hsw(0).start()
    hb1().wait_recv()
    for d in Y_ALL:
        hb2(d).start()
    tail_h().wait_recv()
    m.gs[...] = m.gxa[xh, :, :, :HALF] + m.gxr[...].astype(F32)
    m.gsb[...] = m.gs[...].astype(BF16)
    for d in Z_ORDER:
        tail_z1(d).start()
    each((backward_w, 0))
    ha2().wait_recv()
    hsw(1).start()
    for d in Y_ALL:
        hb2(d).wait_recv()
    hsw(2).start()
    total = m.gxa[:, z, :, HALF:]
    for d in Z_ORDER:
        tail_z2(d).wait_recv()
        total = total + m.gz2[d - 1].astype(F32)
    m.es[...] = total
    tail_h2().start()
    for part in range(3):
        hsw(part).wait_recv()
    each((backward_d, 0))
    total = m.gs[z]
    for d in Z_ORDER:
        tail_z1(d).wait_recv()
        total = total + m.gz1[d - 1].astype(F32)
    gx_ref[:, :HALF] = total.astype(BF16)
    tail_h2().wait_recv()
    gx_ref[:, HALF:] = (m.es[xh] + m.esr[...]).astype(BF16)

    sent = [send_w(j) for j in range(3)] + [dy_h(), swap_x(0), swap_x(1), swap_dy()]
    sent += [c(d) for c in (x_z, dy_z, tail_z1, tail_z2) for d in range(1, NZ)]
    sent += [x_h(d) for d in range(NZ)] + [tail_h(), tail_h2()]
    sent += [c(d) for c in (ha1, hb2) for d in Y_ALL] + [ha2(), hb1()] + [hsw(p) for p in range(3)]
    for c in sent:
        c.wait_send()

    def drain(i, _):
        sent = up_stream.sent(i) + dy_stream.sent(i) + [ga2(i), gb1(i)]
        sent += [ga1(i, d) for d in Y_ALL] + [g(i, w) for g in (gb2, gb3) for w in range(2)]
        sent += [sw(i, part) for part in range(3)]
        for c in sent:
            c.wait_send()
        return 0

    lax.fori_loop(0, CHUNKS, drain, 0)


def writer(gx, outs, gx_out, gg_out, gu_out, gd_out, sems):
    copies = [
        pltpu.make_async_copy(outs.at[:, :, pl.ds(ROWS * j, ROWS)], dst, sems.at[j])
        for j, dst in enumerate((gg_out, gu_out, gd_out))
    ]
    copies.append(pltpu.make_async_copy(gx, gx_out, sems.at[3]))
    for c in copies:
        c.start()
    for c in copies:
        c.wait()


def per_device(x_rows, grad_out, order, gate_t, up_t, down_w):
    any_spec = pl.BlockSpec(memory_space=pl.ANY)
    hbm_spec = pl.BlockSpec(memory_space=pltpu.HBM)
    vmem_spec = pl.BlockSpec(memory_space=pltpu.VMEM)
    dma = pltpu.SemaphoreType.DMA
    held = pl.pallas_call(
        kernel,
        out_shape=[pltpu.VMEM((TB, WIDE), BF16), pltpu.VMEM((2, CHUNKS, 3 * ROWS, WIDE), BF16)],
        in_specs=[hbm_spec, hbm_spec, vmem_spec] + [hbm_spec] * 3,
        out_specs=[vmem_spec] * 2,
        scratch_shapes=[
            dma(shape) if dtype is None else pltpu.VMEM(shape, dtype)
            for _, shape, dtype in scratch_plan()
        ],
        compiler_params=pltpu.CompilerParams(
            collective_id=0, has_side_effects=True, vmem_limit_bytes=57 * 2**20
        ),
        name="ffn_backward",
    )(
        x_rows, grad_out, order.reshape(1, TOK),
        gate_t.reshape(WEIGHT), up_t.reshape(WEIGHT), down_w.reshape(WEIGHT),
    )
    out = pl.pallas_call(
        writer,
        out_shape=[jax.ShapeDtypeStruct((TB, WIDE), BF16)]
        + [jax.ShapeDtypeStruct(WEIGHT, BF16)] * 3,
        in_specs=[vmem_spec] * 2,
        out_specs=[any_spec] * 4,
        scratch_shapes=[dma((4,))],
        compiler_params=pltpu.CompilerParams(vmem_limit_bytes=4 * 2**20),
        name="write_results",
    )(*held)
    full = gate_t.shape
    return out[0], out[1].reshape(full), out[2].reshape(full), out[3].reshape(full)


def solution(mesh):
    return jax.shard_map(
        per_device,
        mesh=mesh,
        in_specs=(
            P("tensor", "dp"),
            P("tensor", "dp"),
            P(),
            P("tensor", "dp"),
            P("tensor", "dp"),
            P("tensor", "dp"),
        ),
        out_specs=(P("tensor", "dp"), P("tensor", "dp"), P("tensor", "dp"), P("tensor", "dp")),
        check_vma=False,
    )
```

```python
from types import SimpleNamespace

import jax
import jax.numpy as jnp
from jax import lax
from jax.experimental import pallas as pl
from jax.experimental.pallas import tpu as pltpu
from jax.sharding import PartitionSpec as P

MESH = pl.DeviceIdType.MESH
NY, NXL, NXH, NZ = 4, 2, 2, 8
CHUNKS = 7
ROWS = 128
SUB = 16
HALF = 256
TOK = 512
WIDE = 512
TB = 32
F32, BF16 = jnp.float32, jnp.bfloat16
Z_ORDER = (1, 7, 2, 6, 3, 5, 4)
Y_ALL = (1, 3, 2)
WEIGHT = (2, CHUNKS, ROWS, WIDE)


def dot_nt(a, b):
    return lax.dot_general(a, b, (((1,), (1,)), ((), ())), preferred_element_type=F32)


def dot_nn(a, b):
    return lax.dot_general(a, b, (((1,), (0,)), ((), ())), preferred_element_type=F32)


def dot_tn(a, b):
    return lax.dot_general(a, b, (((0,), (0,)), ((), ())), preferred_element_type=F32)


def scratch_plan():
    n = CHUNKS
    cell = (SUB, HALF)
    plan = [
        ("wall", (2, n, 3 * ROWS, WIDE), BF16),
        ("wsib", (n, 3 * ROWS, WIDE), BF16),
        ("xo", (NXH, NZ, TB, WIDE), BF16),
        ("xs", (NXH, NZ, TB, WIDE), BF16),
        ("dg", (NXH, NZ, TB, WIDE), BF16),
        ("do", (NXH, NZ, TB, WIDE), BF16),
        ("ds", (NXH, NZ, TB, WIDE), BF16),
        ("place", (TOK, TOK), BF16),
    ]
    for s, nf in (("u", 2), ("d", 1)):
        grid = (n, nf, NXL, NY) + cell
        plan += [
            (s + "_pf_a", grid, F32),
            (s + "_pf_b", grid, F32),
            (s + "_pb_a", grid, BF16),
            (s + "_pb_b", grid, BF16),
            (s + "_rx_a", (n, nf, NY) + cell, BF16),
            (s + "_sb_a", (n, nf, NY) + cell, BF16),
            (s + "_ry_a", (n, 3, nf) + cell, BF16),
            (s + "_r0_b", (n, 2, nf) + cell, BF16),
            (s + "_f_b", (n, 2, nf, NXL) + cell, BF16),
            (s + "_r1_b", (n, 2, nf, NXL) + cell, BF16),
            (s + "_s_b", (n, nf, NXL) + cell, F32),
            (s + "_sb_b", (n, nf) + cell, BF16),
            (s + "_rx_b", (n, nf) + cell, BF16),
            (s + "_send", (n, 9), None),
            (s + "_recv", (n, 9), None),
        ]
    plan += [
        ("t_a", (n, 2) + cell, F32),
        ("t_b", (n, 2) + cell, F32),
        ("g_a", (2, n, 2, NXL, NY) + cell, BF16),
        ("g_b", (2, n, 2, NXL, NY) + cell, BF16),
        ("h_a", (2, n, NXL, NY) + cell, BF16),
        ("h_b", (2, n, NXL, NY) + cell, BF16),
        ("gxa", (NXH, NZ, TB, WIDE), F32),
        ("es", (NXH, TB, HALF), F32),
        ("esr", (TB, HALF), F32),
        ("gxb", (2, NXH, NZ, TB, HALF), BF16),
        ("gxr", (NZ, TB, HALF), BF16),
        ("gs", (NZ, TB, HALF), F32),
        ("gsb", (NZ, TB, HALF), BF16),
        ("gz1", (NZ - 1, TB, HALF), BF16),
        ("gz2", (NZ - 1, NXH, TB, HALF), BF16),
        ("g_send", (n, 12), None),
        ("g_recv", (n, 12), None),
        ("h_send", (11,), None),
        ("h_recv", (11,), None),
        ("w_send", (3,), None),
        ("w_recv", (3,), None),
        ("l_sem", (5,), None),
        ("xz_send", (2, NZ), None),
        ("xz_recv", (2, NZ), None),
        ("xh_send", (NZ + 1,), None),
        ("xh_recv", (NZ + 1,), None),
        ("sib_send", (3,), None),
        ("sib_recv", (3,), None),
        ("t_send", (2 * NZ,), None),
        ("t_recv", (2 * NZ,), None),
    ]
    return plan


def kernel(x_hbm, dy_hbm, order_ref, wg, wu, wd, gx_ref, outs, *scratch):
    m = SimpleNamespace(**{p[0]: ref for p, ref in zip(scratch_plan(), scratch)})
    dp = lax.axis_index("dp")
    tn = lax.axis_index("tensor")
    y, xl, k = dp // 4, (dp // 2) % 2, dp % 2
    xh, z = tn // NZ, tn % NZ

    def at(yy, xx, kk, hh, zz):
        return (yy * 4 + xx * 2 + kk, hh * NZ + zz)

    sibling = at(y, xl, 1 - k, xh, z)
    x_peer = at(y, 1 - xl, k, xh, z)
    h_peer = at(y, xl, k, 1 - xh, z)

    def y_at(d):
        return (y + d) % NY

    def y_peer(d):
        return at(y_at(d), xl, k, xh, z)

    def z_peer(d):
        return at(y, xl, k, xh, (z + d) % NZ)

    def rc(src, dst, send, recv, dev):
        return pltpu.make_async_remote_copy(
            src_ref=src, dst_ref=dst, send_sem=send, recv_sem=recv, device_id=dev, device_id_type=MESH
        )

    def load_w(j):
        return pltpu.make_async_copy(
            (wg, wu, wd)[j], m.wall.at[:, :, pl.ds(ROWS * j, ROWS)], m.l_sem.at[j]
        )

    def send_w(j):
        dst = m.wsib.at[:, pl.ds(ROWS * j, ROWS)]
        return rc((wg, wu, wd)[j].at[1 - k], dst, m.w_send.at[j], m.w_recv.at[j], sibling)

    def load_x():
        return pltpu.make_async_copy(x_hbm, m.xo.at[0, z], m.l_sem.at[3])

    def load_dy():
        return pltpu.make_async_copy(dy_hbm, m.dg.at[xh, z], m.l_sem.at[4])

    def x_z(d):
        return rc(x_hbm, m.xo.at[0, z], m.xz_send.at[0, d], m.xz_recv.at[0, d], z_peer(d))

    def x_h(d):
        at_z = (z + NZ - d) % NZ
        return rc(m.xo.at[0, at_z], m.xo.at[1, at_z], m.xh_send.at[d], m.xh_recv.at[d], h_peer)

    def dy_h():
        return rc(dy_hbm, m.dg.at[xh, z], m.xh_send.at[NZ], m.xh_recv.at[NZ], h_peer)

    def dy_z(d):
        pair = m.dg.at[:, z]
        return rc(pair, pair, m.xz_send.at[1, d], m.xz_recv.at[1, d], z_peer(d))

    def swap_x(part):
        return rc(m.xo.at[part], m.xs.at[part], m.sib_send.at[part], m.sib_recv.at[part], sibling)

    def swap_dy():
        return rc(m.do, m.ds, m.sib_send.at[2], m.sib_recv.at[2], sibling)

    def stream(s, nf):
        pre = s + "_"
        q = SimpleNamespace(
            **{key[len(pre) :]: ref for key, ref in vars(m).items() if key.startswith(pre)}
        )

        def cc(i, c, src, dst, dev):
            return rc(src, dst, q.send.at[i, c], q.recv.at[i, c], dev)

        def a1(i):
            return cc(i, 0, q.pb_a.at[i, :, 1 - xl], q.rx_a.at[i], x_peer)

        def a2(i, d):
            return cc(i, d, q.sb_a.at[i, :, y_at(d)], q.ry_a.at[i, d - 1], y_peer(d))

        def b0(i, w):
            return cc(i, 4 + w, q.pb_b.at[i, :, w, y_at(2)], q.r0_b.at[i, w], y_peer((1, 3)[w]))

        def b1(i, w):
            return cc(i, 6 + w, q.f_b.at[i, w], q.r1_b.at[i, w], y_peer((1, 3)[w]))

        def b2(i):
            return cc(i, 8, q.sb_b.at[i], q.rx_b.at[i], x_peer)

        def begin_a(i, part):
            part = part.reshape(nf, NXL, NY, SUB, HALF)
            q.pf_a[i] = part
            q.pb_a[i] = part.astype(BF16)
            a1(i).start()

        def begin_b(i, part):
            part = part.reshape(nf, NXL, NY, SUB, HALF)
            q.pf_b[i] = part
            q.pb_b[i] = part.astype(BF16)
            for w in range(2):
                b0(i, w).start()

        def first(i):
            for w in range(2):
                b0(i, w).wait_recv()
                to = y_at((1, 3)[w])
                q.f_b[i, w, :, w] = (q.pf_b[i, :, w, to] + q.r0_b[i, w].astype(F32)).astype(BF16)
                q.f_b[i, w, :, 1 - w] = q.pb_b[i, :, 1 - w, to]
                b1(i, w).start()
            a1(i).wait_recv()
            q.sb_a[i] = (q.pf_a[i, :, xl] + q.rx_a[i].astype(F32)).astype(BF16)
            for d in Y_ALL:
                a2(i, d).start()

        def sum_a(i):
            total = q.pf_a[i, :, xl, y] + q.rx_a[i, :, y].astype(F32)
            for d in Y_ALL:
                a2(i, d).wait_recv()
                total = total + q.ry_a[i, d - 1].astype(F32)
            return total

        def second_b(i):
            total = q.pf_b[i, :, :, y]
            for w in range(2):
                b1(i, w).wait_recv()
                total = total + q.r1_b[i, w].astype(F32)
            q.s_b[i] = total
            q.sb_b[i] = q.s_b[i, :, 1 - xl].astype(BF16)
            b2(i).start()

        def sum_b(i):
            b2(i).wait_recv()
            return q.s_b[i, :, xl] + q.rx_b[i].astype(F32)

        def sent(i):
            cs = [a1(i), b2(i)] + [a2(i, d) for d in Y_ALL]
            return cs + [b(i, w) for b in (b0, b1) for w in range(2)]

        return SimpleNamespace(
            begin_a=begin_a, begin_b=begin_b, first=first, sum_a=sum_a, second_b=second_b, sum_b=sum_b, sent=sent
        )

    up_stream, dy_stream = stream("u", 2), stream("d", 1)

    def cg(i, c, src, dev):
        return rc(src, src, m.g_send.at[i, c], m.g_recv.at[i, c], dev)

    def ga1(i, d):
        return cg(i, d - 1, m.g_a.at[k, i, :, xl, y], y_peer(d))

    def ga2(i):
        return cg(i, 3, m.g_a.at[k, i, :, xl], x_peer)

    def gb1(i):
        return cg(i, 4, m.g_b.at[k, i, :, xl, y], x_peer)

    def gb2(i, w):
        return cg(i, 5 + w, m.g_b.at[k, i, :, :, y], y_peer((1, 3)[w]))

    def gb3(i, w):
        return cg(i, 7 + w, m.g_b.at[k, i, :, w, y_at((3, 1)[w])], y_peer((1, 3)[w]))

    def sw(i, part):
        src = (m.g_a.at[k, i, :, xl], m.g_a.at[k, i, :, 1 - xl], m.g_b.at[k, i])[part]
        return cg(i, 9 + part, src, sibling)

    def ch(c, src, dev):
        return rc(src, src, m.h_send.at[c], m.h_recv.at[c], dev)

    def ha1(d):
        return ch(d - 1, m.h_a.at[k, :, xl, y], y_peer(d))

    def ha2():
        return ch(3, m.h_a.at[k, :, xl], x_peer)

    def hb1():
        return ch(4, m.h_b.at[k, :, xl, y], x_peer)

    def hb2(d):
        return ch(4 + d, m.h_b.at[k, :, :, y], y_peer(d))

    def hsw(part):
        src = (m.h_a.at[k, :, xl], m.h_a.at[k, :, 1 - xl], m.h_b.at[k])[part]
        return ch(8 + part, src, sibling)

    def ct(c, src, dst, dev):
        return rc(src, dst, m.t_send.at[c], m.t_recv.at[c], dev)

    def tail_h():
        return ct(0, m.gxb.at[0, 1], m.gxr, h_peer)

    def tail_z1(d):
        return ct(d, m.gsb.at[(z + d) % NZ], m.gz1.at[d - 1], z_peer(d))

    def tail_z2(d):
        return ct(NZ + d, m.gxb.at[1, :, (z + d) % NZ], m.gz2.at[d - 1], z_peer(d))

    def tail_h2():
        return ct(NZ, m.es.at[1], m.esr, h_peer)

    load_x().start()
    load_dy().start()
    for j in range(3):
        load_w(j).start()
    barrier = pltpu.get_barrier_semaphore()
    partners = [z_peer(d) for d in range(1, NZ)] + [y_peer(d) for d in range(1, NY)]
    partners += [h_peer, x_peer, sibling]
    for dev in partners:
        pl.semaphore_signal(barrier, inc=1, device_id=dev, device_id_type=MESH)
    pl.semaphore_wait(barrier, len(partners))

    for d in Z_ORDER:
        x_z(d).start()
    load_x().wait()
    x_h(0).start()
    dy_h().start()
    for j in range(3):
        send_w(j).start()
    m.gxa[...] = jnp.zeros_like(m.gxa)
    rows = (lax.broadcasted_iota(jnp.int32, (TOK, TOK), 0) + xh * HALF) % TOK
    m.place[...] = jnp.where(rows == order_ref[...], 1.0, 0.0).astype(BF16)
    for d in Z_ORDER:
        x_z(d).wait_recv()
        x_h(d).start()
    swap_x(0).start()
    load_dy().wait()
    dy_h().wait_recv()
    for d in Z_ORDER:
        dy_z(d).start()
    for j in range(2):
        load_w(j).wait()
        send_w(j).wait_recv()
    swap_x(0).wait_recv()

    def flat(ref):
        return ref[...].reshape(TOK, WIDE)

    def prepare_dy():
        for d in Z_ORDER:
            dy_z(d).wait_recv()
        m.do[...] = dot_nn(m.place[...], flat(m.dg)).astype(BF16).reshape(NXH, NZ, TB, WIDE)
        swap_dy().start()

    def half_of(ref, p):
        return ref[p].reshape(HALF, WIDE)

    def gate_up(i, p):
        own = dot_nt(m.wall[k, i, : 2 * ROWS], half_of(m.xo, p))
        return own + dot_nt(m.wsib[i, : 2 * ROWS], half_of(m.xs, p))

    def forward_ua(i):
        up_stream.begin_a(i, gate_up(i, 0))

    def forward_ub(i):
        up_stream.begin_b(i, gate_up(i, 1))

    def forward_d(i):
        own = dot_nt(m.wall[k, i, 2 * ROWS :], flat(m.do))
        both = own + dot_nt(m.wsib[i, 2 * ROWS :], flat(m.ds))
        dy_stream.begin_a(i, both[:, :HALF])
        dy_stream.begin_b(i, both[:, HALF:])

    def hidden_of(i, total, t, h):
        t[i] = total
        gate, up = total[0], total[1]
        h[k, i, xl, y] = (gate * jax.nn.sigmoid(gate) * up).astype(BF16)

    def second_u(i):
        hidden_of(i, up_stream.sum_a(i), m.t_a, m.h_a)
        up_stream.second_b(i)

    def third_u(i):
        hidden_of(i, up_stream.sum_b(i), m.t_b, m.h_b)

    def gated(i, grad_hidden, t, g):
        gate, up = t[i, 0], t[i, 1]
        sig = jax.nn.sigmoid(gate)
        grad_gate = grad_hidden * up * sig * (1.0 + gate * (1.0 - sig))
        grad_up = grad_hidden * (gate * sig)
        g[k, i, 0, xl, y] = grad_gate.astype(BF16)
        g[k, i, 1, xl, y] = grad_up.astype(BF16)

    def second_d(i):
        gated(i, dy_stream.sum_a(i)[0], m.t_a, m.g_a)
        for d in Y_ALL:
            ga1(i, d).start()
        dy_stream.second_b(i)

    def third_d(i):
        gated(i, dy_stream.sum_b(i)[0], m.t_b, m.g_b)
        gb1(i).start()

    def gather_a1(i):
        for d in Y_ALL:
            ga1(i, d).wait_recv()
        ga2(i).start()
        sw(i, 0).start()

    def gather_b1(i):
        gb1(i).wait_recv()
        for w in range(2):
            gb2(i, w).start()

    def gather_a2(i):
        ga2(i).wait_recv()
        sw(i, 1).start()

    def gather_b2(i):
        for w in range(2):
            gb2(i, w).wait_recv()
            gb3(i, w).start()

    def gather_b3(i):
        for w in range(2):
            gb3(i, w).wait_recv()
        sw(i, 2).start()

    def backward(i, p, g):
        for h in range(2):
            m.gxa[p] += dot_tn(
                g[h, i].reshape(2 * ROWS, HALF), m.wall[h, i, : 2 * ROWS]
            ).reshape(NZ, TB, WIDE)

    def backward_a(i):
        for part in range(2):
            sw(i, part).wait_recv()
        backward(i, 0, m.g_a)

    def backward_b(i):
        sw(i, 2).wait_recv()
        backward(i, 1, m.g_b)

    def backward_w(i):
        for h in range(2):
            gu = dot_nn(m.g_a[h, i].reshape(2 * ROWS, HALF), m.xo[0].reshape(HALF, WIDE))
            gu = gu + dot_nn(m.g_b[h, i].reshape(2 * ROWS, HALF), m.xo[1].reshape(HALF, WIDE))
            outs[h, i, : 2 * ROWS] = gu.astype(BF16)

    def backward_d(i):
        for h in range(2):
            gd = dot_nn(m.h_a[h, i].reshape(ROWS, HALF), m.do[0].reshape(HALF, WIDE))
            gd = gd + dot_nn(m.h_b[h, i].reshape(ROWS, HALF), m.do[1].reshape(HALF, WIDE))
            outs[h, i, 2 * ROWS :] = gd.astype(BF16)

    end = CHUNKS - 1

    def each(*steps, lo=0, hi=CHUNKS):
        most = max(lag for _, lag in steps)

        def turn(it, _):
            for step, lag in steps:
                i = it - lag
                if most == 0:
                    step(i)
                    continue

                @pl.when((i >= lo) & (i < hi))
                def _():
                    step(i)

            return 0

        lax.fori_loop(lo, hi + most, turn, 0)

    each((forward_ua, 0))
    for d in range(NZ):
        x_h(d).wait_recv()
    swap_x(1).start()
    swap_x(1).wait_recv()
    each((forward_ub, 0))
    each((up_stream.first, 0), lo=0, hi=5)
    prepare_dy()
    each((up_stream.first, 0), lo=5, hi=CHUNKS)
    load_w(2).wait()
    send_w(2).wait_recv()
    swap_dy().wait_recv()
    each((forward_d, 0))
    each((second_u, 0))
    each((dy_stream.first, 0))
    each((third_u, 0))
    each((second_d, 0))
    for d in Y_ALL:
        ha1(d).start()
    each((third_d, 0))
    each((gather_a1, 0))
    hb1().start()
    each((gather_b1, 0))
    each((gather_b2, 0))
    each((gather_a2, 0))
    each((gather_b3, 0))
    for d in Y_ALL:
        ha1(d).wait_recv()
    ha2().start()
    hsw(0).start()
    hb1().wait_recv()
    for d in Y_ALL:
        hb2(d).start()
    each((backward_a, 0))
    each((backward_b, 0))
    m.gxb[0] = m.gxa[:, :, :, :HALF].astype(BF16)
    m.gxb[1] = m.gxa[:, :, :, HALF:].astype(BF16)
    tail_h().start()
    for d in Z_ORDER:
        tail_z2(d).start()
    tail_h().wait_recv()
    m.gs[...] = m.gxa[0, :, :, :HALF] + m.gxr[...].astype(F32)
    m.gsb[...] = m.gs[...].astype(BF16)
    for d in Z_ORDER:
        tail_z1(d).start()
    each((backward_w, 0))
    ha2().wait_recv()
    hsw(1).start()
    for d in Y_ALL:
        hb2(d).wait_recv()
    hsw(2).start()
    total = m.gxa[:, z, :, HALF:]
    for d in Z_ORDER:
        tail_z2(d).wait_recv()
        total = total + m.gz2[d - 1].astype(F32)
    m.es[...] = total
    tail_h2().start()
    for part in range(3):
        hsw(part).wait_recv()
    each((backward_d, 0))
    total = m.gs[z]
    for d in Z_ORDER:
        tail_z1(d).wait_recv()
        total = total + m.gz1[d - 1].astype(F32)
    gx_ref[:, :HALF] = total.astype(BF16)
    tail_h2().wait_recv()
    gx_ref[:, HALF:] = (m.es[0] + m.esr[...]).astype(BF16)

    sent = [send_w(j) for j in range(3)] + [dy_h(), swap_x(0), swap_x(1), swap_dy()]
    sent += [c(d) for c in (x_z, dy_z, tail_z1, tail_z2) for d in range(1, NZ)]
    sent += [x_h(d) for d in range(NZ)] + [tail_h(), tail_h2()]
    sent += [c(d) for c in (ha1, hb2) for d in Y_ALL] + [ha2(), hb1()] + [hsw(p) for p in range(3)]
    for c in sent:
        c.wait_send()

    def drain(i, _):
        sent = up_stream.sent(i) + dy_stream.sent(i) + [ga2(i), gb1(i)]
        sent += [ga1(i, d) for d in Y_ALL] + [g(i, w) for g in (gb2, gb3) for w in range(2)]
        sent += [sw(i, part) for part in range(3)]
        for c in sent:
            c.wait_send()
        return 0

    lax.fori_loop(0, CHUNKS, drain, 0)


def writer(gx, outs, gx_out, gg_out, gu_out, gd_out, sems):
    copies = [
        pltpu.make_async_copy(outs.at[:, :, pl.ds(ROWS * j, ROWS)], dst, sems.at[j])
        for j, dst in enumerate((gg_out, gu_out, gd_out))
    ]
    copies.append(pltpu.make_async_copy(gx, gx_out, sems.at[3]))
    for c in copies:
        c.start()
    for c in copies:
        c.wait()


def per_device(x_rows, grad_out, order, gate_t, up_t, down_w):
    any_spec = pl.BlockSpec(memory_space=pl.ANY)
    hbm_spec = pl.BlockSpec(memory_space=pltpu.HBM)
    vmem_spec = pl.BlockSpec(memory_space=pltpu.VMEM)
    dma = pltpu.SemaphoreType.DMA
    held = pl.pallas_call(
        kernel,
        out_shape=[pltpu.VMEM((TB, WIDE), BF16), pltpu.VMEM((2, CHUNKS, 3 * ROWS, WIDE), BF16)],
        in_specs=[hbm_spec, hbm_spec, vmem_spec] + [hbm_spec] * 3,
        out_specs=[vmem_spec] * 2,
        scratch_shapes=[
            dma(shape) if dtype is None else pltpu.VMEM(shape, dtype)
            for _, shape, dtype in scratch_plan()
        ],
        compiler_params=pltpu.CompilerParams(
            collective_id=0, has_side_effects=True, vmem_limit_bytes=57 * 2**20
        ),
        name="ffn_backward",
    )(
        x_rows, grad_out, order.reshape(1, TOK),
        gate_t.reshape(WEIGHT), up_t.reshape(WEIGHT), down_w.reshape(WEIGHT),
    )
    out = pl.pallas_call(
        writer,
        out_shape=[jax.ShapeDtypeStruct((TB, WIDE), BF16)]
        + [jax.ShapeDtypeStruct(WEIGHT, BF16)] * 3,
        in_specs=[vmem_spec] * 2,
        out_specs=[any_spec] * 4,
        scratch_shapes=[dma((4,))],
        compiler_params=pltpu.CompilerParams(vmem_limit_bytes=4 * 2**20),
        name="write_results",
    )(*held)
    full = gate_t.shape
    return out[0], out[1].reshape(full), out[2].reshape(full), out[3].reshape(full)


def solution(mesh):
    return jax.shard_map(
        per_device,
        mesh=mesh,
        in_specs=(
            P("tensor", "dp"),
            P("tensor", "dp"),
            P(),
            P("tensor", "dp"),
            P("tensor", "dp"),
            P("tensor", "dp"),
        ),
        out_specs=(P("tensor", "dp"), P("tensor", "dp"), P("tensor", "dp"), P("tensor", "dp")),
        check_vma=False,
    )
```

```python
from types import SimpleNamespace

import jax
import jax.numpy as jnp
from jax import lax
from jax.experimental import pallas as pl
from jax.experimental.pallas import tpu as pltpu
from jax.sharding import PartitionSpec as P

MESH = pl.DeviceIdType.MESH
NY, NXL, NXH, NZ = 4, 2, 2, 8
CHUNKS = 7
ROWS = 128
SUB = 16
HALF = 256
TOK = 512
WIDE = 512
TB = 32
F32, BF16 = jnp.float32, jnp.bfloat16
Z_ORDER = (1, 7, 2, 6, 3, 5, 4)
Y_ALL = (1, 3, 2)
WEIGHT = (2, CHUNKS, ROWS, WIDE)


def dot_nt(a, b):
    return lax.dot_general(a, b, (((1,), (1,)), ((), ())), preferred_element_type=F32)


def dot_nn(a, b):
    return lax.dot_general(a, b, (((1,), (0,)), ((), ())), preferred_element_type=F32)


def dot_tn(a, b):
    return lax.dot_general(a, b, (((0,), (0,)), ((), ())), preferred_element_type=F32)


def scratch_plan():
    n = CHUNKS
    cell = (SUB, HALF)
    plan = [
        ("wall", (2, n, 3 * ROWS, WIDE), BF16),
        ("wsib", (n, 3 * ROWS, WIDE), BF16),
        ("xo", (NXH, NZ, TB, WIDE), BF16),
        ("xs", (NXH, NZ, TB, WIDE), BF16),
        ("dg", (NXH, NZ, TB, WIDE), BF16),
        ("do", (NXH, NZ, TB, WIDE), BF16),
        ("ds", (NXH, NZ, TB, WIDE), BF16),
        ("place", (TOK, TOK), BF16),
    ]
    for s, nf in (("u", 2), ("d", 1)):
        grid = (n, nf, NXL, NY) + cell
        plan += [
            (s + "_pf_a", grid, F32),
            (s + "_pf_b", grid, F32),
            (s + "_pb_a", grid, BF16),
            (s + "_pb_b", grid, BF16),
            (s + "_rx_a", (n, nf, NY) + cell, BF16),
            (s + "_sb_a", (n, nf, NY) + cell, BF16),
            (s + "_ry_a", (n, 3, nf) + cell, BF16),
            (s + "_r0_b", (n, 2, nf) + cell, BF16),
            (s + "_f_b", (n, 2, nf, NXL) + cell, BF16),
            (s + "_r1_b", (n, 2, nf, NXL) + cell, BF16),
            (s + "_s_b", (n, nf, NXL) + cell, F32),
            (s + "_sb_b", (n, nf) + cell, BF16),
            (s + "_rx_b", (n, nf) + cell, BF16),
            (s + "_send", (n, 9), None),
            (s + "_recv", (n, 9), None),
        ]
    plan += [
        ("t_a", (n, 2) + cell, F32),
        ("t_b", (n, 2) + cell, F32),
        ("g_a", (2, n, 2, NXL, NY) + cell, BF16),
        ("g_b", (2, n, 2, NXL, NY) + cell, BF16),
        ("h_a", (2, n, NXL, NY) + cell, BF16),
        ("h_b", (2, n, NXL, NY) + cell, BF16),
        ("gxa", (NXH, NZ, TB, WIDE), F32),
        ("es", (NXH, TB, HALF), F32),
        ("esr", (TB, HALF), F32),
        ("gxb", (2, NXH, NZ, TB, HALF), BF16),
        ("gxr", (NZ, TB, HALF), BF16),
        ("gs", (NZ, TB, HALF), F32),
        ("gsb", (NZ, TB, HALF), BF16),
        ("gz1", (NZ - 1, TB, HALF), BF16),
        ("gz2", (NZ - 1, NXH, TB, HALF), BF16),
        ("g_send", (n, 12), None),
        ("g_recv", (n, 12), None),
        ("h_send", (11,), None),
        ("h_recv", (11,), None),
        ("w_send", (3,), None),
        ("w_recv", (3,), None),
        ("l_sem", (5,), None),
        ("xz_send", (2, NZ), None),
        ("xz_recv", (2, NZ), None),
        ("xh_send", (NZ + 1,), None),
        ("xh_recv", (NZ + 1,), None),
        ("sib_send", (3,), None),
        ("sib_recv", (3,), None),
        ("t_send", (2 * NZ,), None),
        ("t_recv", (2 * NZ,), None),
    ]
    return plan


def kernel(x_hbm, dy_hbm, order_ref, wg, wu, wd, gx_ref, outs, *scratch):
    m = SimpleNamespace(**{p[0]: ref for p, ref in zip(scratch_plan(), scratch)})
    dp = lax.axis_index("dp")
    tn = lax.axis_index("tensor")
    y, xl, k = dp // 4, (dp // 2) % 2, dp % 2
    xh, z = tn // NZ, tn % NZ

    def at(yy, xx, kk, hh, zz):
        return (yy * 4 + xx * 2 + kk, hh * NZ + zz)

    sibling = at(y, xl, 1 - k, xh, z)
    x_peer = at(y, 1 - xl, k, xh, z)
    h_peer = at(y, xl, k, 1 - xh, z)

    other = 1 - xl
    y_row = [lax.rem(y + d, NY) for d in range(NY)]
    y_dev = [at(row, xl, k, xh, z) for row in y_row]
    z_row = [lax.rem(z + d, NZ) for d in range(NZ)]
    z_dev = [at(y, xl, k, xh, row) for row in z_row]

    def y_at(d):
        return y_row[d % NY]

    def y_peer(d):
        return y_dev[d % NY]

    def z_peer(d):
        return z_dev[d % NZ]

    def rc(src, dst, send, recv, dev):
        return pltpu.make_async_remote_copy(
            src_ref=src, dst_ref=dst, send_sem=send, recv_sem=recv, device_id=dev, device_id_type=MESH
        )

    def load_w(j):
        return pltpu.make_async_copy(
            (wg, wu, wd)[j], m.wall.at[:, :, pl.ds(ROWS * j, ROWS)], m.l_sem.at[j]
        )

    def send_w(j):
        dst = m.wsib.at[:, pl.ds(ROWS * j, ROWS)]
        return rc((wg, wu, wd)[j].at[1 - k], dst, m.w_send.at[j], m.w_recv.at[j], sibling)

    def load_x():
        return pltpu.make_async_copy(x_hbm, m.xo.at[0, z], m.l_sem.at[3])

    def load_dy():
        return pltpu.make_async_copy(dy_hbm, m.dg.at[xh, z], m.l_sem.at[4])

    def x_z(d):
        return rc(x_hbm, m.xo.at[0, z], m.xz_send.at[0, d], m.xz_recv.at[0, d], z_peer(d))

    def x_h(d):
        at_z = z_row[(NZ - d) % NZ]
        return rc(m.xo.at[0, at_z], m.xo.at[1, at_z], m.xh_send.at[d], m.xh_recv.at[d], h_peer)

    def dy_h():
        return rc(dy_hbm, m.dg.at[xh, z], m.xh_send.at[NZ], m.xh_recv.at[NZ], h_peer)

    def dy_z(d):
        pair = m.dg.at[:, z]
        return rc(pair, pair, m.xz_send.at[1, d], m.xz_recv.at[1, d], z_peer(d))

    def swap_x(part):
        return rc(m.xo.at[part], m.xs.at[part], m.sib_send.at[part], m.sib_recv.at[part], sibling)

    def swap_dy():
        return rc(m.do, m.ds, m.sib_send.at[2], m.sib_recv.at[2], sibling)

    def stream(s, nf):
        pre = s + "_"
        q = SimpleNamespace(
            **{key[len(pre) :]: ref for key, ref in vars(m).items() if key.startswith(pre)}
        )

        def cc(i, c, src, dst, dev):
            return rc(src, dst, q.send.at[i, c], q.recv.at[i, c], dev)

        def a1(i):
            return cc(i, 0, q.pb_a.at[i, :, other], q.rx_a.at[i], x_peer)

        def a2(i, d):
            return cc(i, d, q.sb_a.at[i, :, y_at(d)], q.ry_a.at[i, d - 1], y_peer(d))

        def b0(i, w):
            return cc(i, 4 + w, q.pb_b.at[i, :, w, y_at(2)], q.r0_b.at[i, w], y_peer((1, 3)[w]))

        def b1(i, w):
            return cc(i, 6 + w, q.f_b.at[i, w], q.r1_b.at[i, w], y_peer((1, 3)[w]))

        def b2(i):
            return cc(i, 8, q.sb_b.at[i], q.rx_b.at[i], x_peer)

        def begin_a(i, part):
            part = part.reshape(nf, NXL, NY, SUB, HALF)
            q.pf_a[i] = part
            q.pb_a[i] = part.astype(BF16)
            a1(i).start()

        def begin_b(i, part):
            part = part.reshape(nf, NXL, NY, SUB, HALF)
            q.pf_b[i] = part
            q.pb_b[i] = part.astype(BF16)
            for w in range(2):
                b0(i, w).start()

        def first(i):
            a1(i).wait_recv()
            q.sb_a[i] = (q.pf_a[i, :, xl] + q.rx_a[i].astype(F32)).astype(BF16)
            for d in Y_ALL:
                a2(i, d).start()
            for w in range(2):
                b0(i, w).wait_recv()
                to = y_at((1, 3)[w])
                q.f_b[i, w, :, w] = (q.pf_b[i, :, w, to] + q.r0_b[i, w].astype(F32)).astype(BF16)
                q.f_b[i, w, :, 1 - w] = q.pb_b[i, :, 1 - w, to]
                b1(i, w).start()

        def sum_a(i):
            total = q.pf_a[i, :, xl, y] + q.rx_a[i, :, y].astype(F32)
            for d in Y_ALL:
                a2(i, d).wait_recv()
                total = total + q.ry_a[i, d - 1].astype(F32)
            return total

        def second_b(i):
            total = q.pf_b[i, :, :, y]
            for w in range(2):
                b1(i, w).wait_recv()
                total = total + q.r1_b[i, w].astype(F32)
            q.s_b[i] = total
            q.sb_b[i] = q.s_b[i, :, other].astype(BF16)
            b2(i).start()

        def sum_b(i):
            b2(i).wait_recv()
            return q.s_b[i, :, xl] + q.rx_b[i].astype(F32)

        def sent(i):
            cs = [a1(i), b2(i)] + [a2(i, d) for d in Y_ALL]
            return cs + [b(i, w) for b in (b0, b1) for w in range(2)]

        return SimpleNamespace(
            begin_a=begin_a, begin_b=begin_b, first=first, sum_a=sum_a, second_b=second_b, sum_b=sum_b, sent=sent
        )

    up_stream, dy_stream = stream("u", 2), stream("d", 1)

    def cg(i, c, src, dev):
        return rc(src, src, m.g_send.at[i, c], m.g_recv.at[i, c], dev)

    def ga1(i, d):
        return cg(i, d - 1, m.g_a.at[k, i, :, xl, y], y_peer(d))

    def ga2(i):
        return cg(i, 3, m.g_a.at[k, i, :, xl], x_peer)

    def gb1(i):
        return cg(i, 4, m.g_b.at[k, i, :, xl, y], x_peer)

    def gb2(i, w):
        return cg(i, 5 + w, m.g_b.at[k, i, :, :, y], y_peer((1, 3)[w]))

    def gb3(i, w):
        return cg(i, 7 + w, m.g_b.at[k, i, :, w, y_at((3, 1)[w])], y_peer((1, 3)[w]))

    def sw(i, part):
        src = (m.g_a.at[k, i, :, xl], m.g_a.at[k, i, :, other], m.g_b.at[k, i])[part]
        return cg(i, 9 + part, src, sibling)

    def ch(c, src, dev):
        return rc(src, src, m.h_send.at[c], m.h_recv.at[c], dev)

    def ha1(d):
        return ch(d - 1, m.h_a.at[k, :, xl, y], y_peer(d))

    def ha2():
        return ch(3, m.h_a.at[k, :, xl], x_peer)

    def hb1():
        return ch(4, m.h_b.at[k, :, xl, y], x_peer)

    def hb2(d):
        return ch(4 + d, m.h_b.at[k, :, :, y], y_peer(d))

    def hsw(part):
        src = (m.h_a.at[k, :, xl], m.h_a.at[k, :, other], m.h_b.at[k])[part]
        return ch(8 + part, src, sibling)

    def ct(c, src, dst, dev):
        return rc(src, dst, m.t_send.at[c], m.t_recv.at[c], dev)

    def tail_h():
        return ct(0, m.gxb.at[0, 1], m.gxr, h_peer)

    def tail_z1(d):
        return ct(d, m.gsb.at[z_row[d]], m.gz1.at[d - 1], z_peer(d))

    def tail_z2(d):
        return ct(NZ + d, m.gxb.at[1, :, z_row[d]], m.gz2.at[d - 1], z_peer(d))

    def tail_h2():
        return ct(NZ, m.es.at[1], m.esr, h_peer)

    load_x().start()
    load_dy().start()
    for j in range(3):
        load_w(j).start()
    barrier = pltpu.get_barrier_semaphore()
    partners = [z_peer(d) for d in range(1, NZ)] + [y_peer(d) for d in range(1, NY)]
    partners += [h_peer, x_peer, sibling]
    for dev in partners:
        pl.semaphore_signal(barrier, inc=1, device_id=dev, device_id_type=MESH)
    pl.semaphore_wait(barrier, len(partners))

    for d in Z_ORDER:
        x_z(d).start()
    load_x().wait()
    x_h(0).start()
    dy_h().start()
    for j in range(3):
        send_w(j).start()
    m.gxa[...] = jnp.zeros_like(m.gxa)
    rows = (lax.broadcasted_iota(jnp.int32, (TOK, TOK), 0) + xh * HALF) % TOK
    m.place[...] = jnp.where(rows == order_ref[...], 1.0, 0.0).astype(BF16)
    for d in Z_ORDER:
        x_z(d).wait_recv()
        x_h(d).start()
    swap_x(0).start()
    load_dy().wait()
    dy_h().wait_recv()
    for d in Z_ORDER:
        dy_z(d).start()
    for j in range(2):
        load_w(j).wait()
        send_w(j).wait_recv()
    swap_x(0).wait_recv()

    def flat(ref):
        return ref[...].reshape(TOK, WIDE)

    def prepare_dy():
        for d in Z_ORDER:
            dy_z(d).wait_recv()
        m.do[...] = dot_nn(m.place[...], flat(m.dg)).astype(BF16).reshape(NXH, NZ, TB, WIDE)
        swap_dy().start()

    def half_of(ref, p):
        return ref[p].reshape(HALF, WIDE)

    def gate_up(i, p):
        own = dot_nt(m.wall[k, i, : 2 * ROWS], half_of(m.xo, p))
        return own + dot_nt(m.wsib[i, : 2 * ROWS], half_of(m.xs, p))

    def forward_ua(i):
        up_stream.begin_a(i, gate_up(i, 0))

    def forward_ub(i):
        up_stream.begin_b(i, gate_up(i, 1))

    def forward_d(i):
        own = dot_nt(m.wall[k, i, 2 * ROWS :], flat(m.do))
        both = own + dot_nt(m.wsib[i, 2 * ROWS :], flat(m.ds))
        dy_stream.begin_a(i, both[:, :HALF])
        dy_stream.begin_b(i, both[:, HALF:])

    def hidden_of(i, total, t, h):
        t[i] = total
        gate, up = total[0], total[1]
        h[k, i, xl, y] = (gate * jax.nn.sigmoid(gate) * up).astype(BF16)

    def second_u(i):
        hidden_of(i, up_stream.sum_a(i), m.t_a, m.h_a)
        up_stream.second_b(i)

    def third_u(i):
        hidden_of(i, up_stream.sum_b(i), m.t_b, m.h_b)

    def gated(i, grad_hidden, t, g):
        gate, up = t[i, 0], t[i, 1]
        sig = jax.nn.sigmoid(gate)
        grad_gate = grad_hidden * up * sig * (1.0 + gate * (1.0 - sig))
        grad_up = grad_hidden * (gate * sig)
        g[k, i, 0, xl, y] = grad_gate.astype(BF16)
        g[k, i, 1, xl, y] = grad_up.astype(BF16)

    def second_d(i):
        dy_stream.second_b(i)
        gated(i, dy_stream.sum_a(i)[0], m.t_a, m.g_a)
        for d in Y_ALL:
            ga1(i, d).start()

    def third_d(i):
        gated(i, dy_stream.sum_b(i)[0], m.t_b, m.g_b)
        gb1(i).start()

    def gather_a1(i):
        for d in Y_ALL:
            ga1(i, d).wait_recv()
        ga2(i).start()
        sw(i, 0).start()

    def gather_b1(i):
        gb1(i).wait_recv()
        for w in range(2):
            gb2(i, w).start()

    def gather_a2(i):
        ga2(i).wait_recv()
        sw(i, 1).start()

    def gather_b2(i):
        for w in range(2):
            gb2(i, w).wait_recv()
            gb3(i, w).start()

    def gather_b3(i):
        for w in range(2):
            gb3(i, w).wait_recv()
        sw(i, 2).start()

    def backward(i, p, g):
        both = [dot_tn(g[h, i].reshape(2 * ROWS, HALF), m.wall[h, i, : 2 * ROWS]) for h in range(2)]
        m.gxa[p] += (both[0] + both[1]).reshape(NZ, TB, WIDE)

    def backward_a(i):
        for part in range(2):
            sw(i, part).wait_recv()
        backward(i, 0, m.g_a)

    def backward_b(i):
        sw(i, 2).wait_recv()
        backward(i, 1, m.g_b)

    def backward_w(i):
        for h in range(2):
            gu = dot_nn(m.g_a[h, i].reshape(2 * ROWS, HALF), m.xo[0].reshape(HALF, WIDE))
            gu = gu + dot_nn(m.g_b[h, i].reshape(2 * ROWS, HALF), m.xo[1].reshape(HALF, WIDE))
            outs[h, i, : 2 * ROWS] = gu.astype(BF16)

    def backward_d(i):
        for h in range(2):
            gd = dot_nn(m.h_a[h, i].reshape(ROWS, HALF), m.do[0].reshape(HALF, WIDE))
            gd = gd + dot_nn(m.h_b[h, i].reshape(ROWS, HALF), m.do[1].reshape(HALF, WIDE))
            outs[h, i, 2 * ROWS :] = gd.astype(BF16)

    end = CHUNKS - 1

    def each(*steps, lo=0, hi=CHUNKS):
        most = max(lag for _, lag in steps)

        def turn(it, _):
            for step, lag in steps:
                i = it - lag
                if most == 0:
                    step(i)
                    continue

                @pl.when((i >= lo) & (i < hi))
                def _():
                    step(i)

            return 0

        lax.fori_loop(lo, hi + most, turn, 0)

    def drain(i, _):
        sent = up_stream.sent(i) + dy_stream.sent(i) + [ga2(i), gb1(i)]
        sent += [ga1(i, d) for d in Y_ALL] + [g(i, w) for g in (gb2, gb3) for w in range(2)]
        sent += [sw(i, part) for part in range(3)]
        for c in sent:
            c.wait_send()
        return 0

    def drain_all():
        sent = [send_w(j) for j in range(3)] + [dy_h(), swap_x(0), swap_x(1), swap_dy()]
        sent += [c(d) for c in (x_z, dy_z) for d in range(1, NZ)] + [x_h(d) for d in range(NZ)]
        sent += [ha1(d) for d in Y_ALL] + [ha2(), hb1()]
        for c in sent:
            c.wait_send()
        lax.fori_loop(0, CHUNKS, drain, 0)

    each((forward_ua, 0))
    for d in range(NZ):
        x_h(d).wait_recv()
    swap_x(1).start()
    swap_x(1).wait_recv()
    each((forward_ub, 0))
    each((up_stream.first, 0), lo=0, hi=5)
    prepare_dy()
    each((up_stream.first, 0), lo=5, hi=CHUNKS)
    load_w(2).wait()
    send_w(2).wait_recv()
    swap_dy().wait_recv()
    each((forward_d, 0))
    each((second_u, 0))
    each((dy_stream.first, 0))
    each((third_u, 0))
    each((second_d, 0))
    for d in Y_ALL:
        ha1(d).start()
    each((third_d, 0))
    each((gather_a1, 0))
    hb1().start()
    each((gather_b1, 0))
    each((gather_b2, 0))
    each((gather_a2, 0))
    each((gather_b3, 0))
    for d in Y_ALL:
        ha1(d).wait_recv()
    ha2().start()
    hsw(0).start()
    hb1().wait_recv()
    for d in Y_ALL:
        hb2(d).start()
    each((backward_a, 0))
    each((backward_b, 0))
    m.gxb[0] = m.gxa[:, :, :, :HALF].astype(BF16)
    m.gxb[1] = m.gxa[:, :, :, HALF:].astype(BF16)
    tail_h().start()
    for d in Z_ORDER:
        tail_z2(d).start()
    tail_h().wait_recv()
    m.gs[...] = m.gxa[0, :, :, :HALF] + m.gxr[...].astype(F32)
    m.gsb[...] = m.gs[...].astype(BF16)
    for d in Z_ORDER:
        tail_z1(d).start()
    each((backward_w, 0))
    ha2().wait_recv()
    hsw(1).start()
    for d in Y_ALL:
        hb2(d).wait_recv()
    hsw(2).start()
    drain_all()
    total = m.gxa[:, z, :, HALF:]
    for d in Z_ORDER:
        tail_z2(d).wait_recv()
        total = total + m.gz2[d - 1].astype(F32)
    m.es[...] = total
    tail_h2().start()
    for part in range(3):
        hsw(part).wait_recv()
    each((backward_d, 0))
    total = m.gs[z]
    for d in Z_ORDER:
        tail_z1(d).wait_recv()
        total = total + m.gz1[d - 1].astype(F32)
    gx_ref[:, :HALF] = total.astype(BF16)
    tail_h2().wait_recv()
    gx_ref[:, HALF:] = (m.es[0] + m.esr[...]).astype(BF16)

    sent = [c(d) for c in (tail_z1, tail_z2) for d in range(1, NZ)] + [tail_h(), tail_h2()]
    sent += [hb2(d) for d in Y_ALL] + [hsw(p) for p in range(3)]
    for c in sent:
        c.wait_send()


def writer(gx, outs, gx_out, gg_out, gu_out, gd_out, sems):
    copies = [
        pltpu.make_async_copy(outs.at[:, :, pl.ds(ROWS * j, ROWS)], dst, sems.at[j])
        for j, dst in enumerate((gg_out, gu_out, gd_out))
    ]
    copies.append(pltpu.make_async_copy(gx, gx_out, sems.at[3]))
    for c in copies:
        c.start()
    for c in copies:
        c.wait()


def per_device(x_rows, grad_out, order, gate_t, up_t, down_w):
    any_spec = pl.BlockSpec(memory_space=pl.ANY)
    hbm_spec = pl.BlockSpec(memory_space=pltpu.HBM)
    vmem_spec = pl.BlockSpec(memory_space=pltpu.VMEM)
    dma = pltpu.SemaphoreType.DMA
    held = pl.pallas_call(
        kernel,
        out_shape=[pltpu.VMEM((TB, WIDE), BF16), pltpu.VMEM((2, CHUNKS, 3 * ROWS, WIDE), BF16)],
        in_specs=[hbm_spec, hbm_spec, vmem_spec] + [hbm_spec] * 3,
        out_specs=[vmem_spec] * 2,
        scratch_shapes=[
            dma(shape) if dtype is None else pltpu.VMEM(shape, dtype)
            for _, shape, dtype in scratch_plan()
        ],
        compiler_params=pltpu.CompilerParams(
            collective_id=0, has_side_effects=True, vmem_limit_bytes=57 * 2**20
        ),
        name="ffn_backward",
    )(
        x_rows, grad_out, order.reshape(1, TOK),
        gate_t.reshape(WEIGHT), up_t.reshape(WEIGHT), down_w.reshape(WEIGHT),
    )
    out = pl.pallas_call(
        writer,
        out_shape=[jax.ShapeDtypeStruct((TB, WIDE), BF16)]
        + [jax.ShapeDtypeStruct(WEIGHT, BF16)] * 3,
        in_specs=[vmem_spec] * 2,
        out_specs=[any_spec] * 4,
        scratch_shapes=[dma((4,))],
        compiler_params=pltpu.CompilerParams(vmem_limit_bytes=4 * 2**20),
        name="write_results",
    )(*held)
    full = gate_t.shape
    return out[0], out[1].reshape(full), out[2].reshape(full), out[3].reshape(full)


def solution(mesh):
    return jax.shard_map(
        per_device,
        mesh=mesh,
        in_specs=(
            P("tensor", "dp"),
            P("tensor", "dp"),
            P(),
            P("tensor", "dp"),
            P("tensor", "dp"),
            P("tensor", "dp"),
        ),
        out_specs=(P("tensor", "dp"), P("tensor", "dp"), P("tensor", "dp"), P("tensor", "dp")),
        check_vma=False,
    )
```
